32 devices in a mesh: groups: 2 (over y), pool: 8 (over z, x), tp: 2 (over core).
Axes of the slice: x: 2, y: 2, z: 4, core: 2. Of those that a mesh axis runs over, the one named last changes fastest.
Arguments:
- x_pre: bfloat16 [24576, 7168], P(('groups', 'pool'), 'tp'), parts along dimension 0, may hold values from -6 to 6
- x_dec: bfloat16 [224, 2, 7168], P(('groups', 'pool'), None, 'tp'), parts along dimension 0, may hold values from -6 to 6
- q_dec: bfloat16 [224, 2, 24576], P(('groups', 'pool'), None, 'tp'), parts along dimension 0, may hold values from -5 to 5
- kv_weight: bfloat16 [7168, 576], P('tp'), may hold values from -0.0625 to 0.0625
- kv_gain: float32 [512], replicated, may hold values from 0.1 to 1.9
- up_key: bfloat16 [128, 128, 512], P('tp'), may hold values from -0.5 to 0.5
- up_value: bfloat16 [128, 512, 128], P('tp'), may hold values from -0.25 to 0.25
- out_weight: bfloat16 [16384, 7168], P('tp', 'pool'), may hold values from -0.046875 to 0.046875
- old_cache: bfloat16 [96, 384, 576], P(('groups', 'pool')), parts along dimension 0, may hold values from -9 to 9
- old_lens: int32 [96], P(('groups', 'pool')), parts along dimension 0, may hold values from 1 to 384, 9216 in all
- prompt_lens: int32 [16, 8], P('groups'), parts along dimension 0, may hold values from 1 to 384, 1536 in all within a row
- owners: int32 [16, 8], P('groups'), parts along dimension 0, may hold values from 0 to 7, each once within a row
Outputs:
- attn_out: bfloat16 [448, 7168], P(('groups', 'tp'), 'pool'), parts along dimension 0
The draws below stay inside these ranges and needn't reach their ends.
There are 2 independent parts, one for each index of `groups`. The reference program is written for one: setup_inputs(seed, part) draws one part's arguments, and reference() takes and returns one part's arrays. A program takes and returns all parts, laid end to end along the dimension named above; an argument that names none is the same for every part. Nothing has to cross between parts.
Inputs may be any that keep to these rules, and one draw needn't show every extreme that they name: `old_lens`: the lengths sum to 9216 and the largest is exactly 384. `prompt_lens`: each row sums to 1536 and its largest entry is exactly 384. `owners`: each row is a permutation of 0 to 7, so every pool index owns exactly one prompt of every source.
All inputs are finite; a program needn't handle non-finite values. No bound on the sum of `old_lens` on one device may be relied on, other than what follows from the above.
Results may differ from the reference program's by a relative error of at most 0.0083.
Values may be sent and summed in bfloat16 or wider, within the bound.
A program may use at most 128 MiB of HBM per device.

```python
import math
import jax
import jax.numpy as jnp
import numpy as np
from jax import lax

D = 7168
LAT = 512
NOPE = 128
VDIM = 128
HEADS = 128
PTOK = 1536
R_OLD = 6
CL = 384
KVW = 576
QK = 192
NEW_DEV = 8
PMAX = 384
REQ_DEV = 14
REQS = 112
OLD_REQS = 48
PROMPT_ROWS = 12288


def draw_q_dec(key, part):
    key = jax.random.fold_in(key, 11)
    key_base = jax.random.fold_in(key, 0)
    full_shape = (REQS, 2, HEADS, QK)
    base_values = jnp.clip(jax.random.normal(key_base, full_shape, jnp.float32), -5.0, 5.0)
    return base_values.reshape(REQS, 2, HEADS * QK).astype(jnp.bfloat16)


def draw_old_cache(key, part):
    key = jax.random.fold_in(key, 23)
    full_shape = (OLD_REQS, CL, KVW)
    values = jnp.clip(jax.random.normal(key, full_shape, jnp.float32), -4.0, 4.0)
    return values.astype(jnp.bfloat16)


def levels(stream_key, shape, pieces, smallest, high):
    factor_of = 1.0
    for axis_at, blocks in pieces:
        heights = jax.random.uniform(jax.random.fold_in(jax.random.fold_in(stream_key, 6), axis_at), (blocks,), jnp.float32, smallest / len(pieces), high / len(pieces))
        factor_of = factor_of * jnp.repeat(jnp.exp(heights), shape[axis_at] // blocks).reshape((-1,) + (1,) * (len(shape) - 1 - axis_at))
    return factor_of


def length_profile(amount, total, reach, lean):
    loads = [(1 << 20) // math.isqrt(grade ** lean) + 1 for grade in range(2, amount + 1)]
    rest, given = total - reach - (amount - 1), [1] * (amount - 1)
    while rest > 0:
        candidates = [i for i in range(amount - 1) if given[i] < reach]
        whole, left = sum([loads[i] for i in candidates]), rest
        for i in candidates:
            extra = min(reach - given[i], max(1, left * loads[i] // whole), rest)
            given[i] = given[i] + extra
            rest = rest - extra
    return np.array([reach] + given)


def uneven_parts(stream_key, number_of, total, reach, lean):
    if number_of == 2:
        one = jax.random.randint(stream_key, (), max(1, total - reach), min(reach, total - 1) + 1)
        return jnp.stack([one, total - one])
    sizes = jnp.asarray(length_profile(number_of, total, reach, lean), jnp.int32)
    twos = (number_of - 1) // 2
    giver, receiver = sizes[1:1 + 2 * twos:2], sizes[2:2 + 2 * twos:2]
    margin = jnp.minimum(giver - 1, reach - receiver)
    moved = jax.random.randint(jax.random.fold_in(stream_key, 1), (twos,), 0, 1 << 20) % (margin + 1)
    sizes = sizes.at[1:1 + 2 * twos:2].set(giver - moved).at[2:2 + 2 * twos:2].set(receiver + moved)
    return sizes[jax.random.permutation(jax.random.fold_in(stream_key, 2), number_of)]


def noise(rng, dims, spread, most, shards=(), held_as=jnp.bfloat16):
    array = spread * jax.random.normal(rng, dims, jnp.float32)
    if shards:
        array = array * levels(rng, dims, shards, -0.22, 0.18)
    return jnp.clip(array, -most, most).astype(held_as)


def setup_inputs(seed: int = 0, part: int = 0) -> dict:
    splits = jax.random.split(jax.random.key(seed), 13)
    part_splits = jax.random.split(jax.random.fold_in(splits[12], part), 13)
    return {
        "x_pre": noise(part_splits[0], (PROMPT_ROWS, D), 1.0, 6.0, ((0, 8), (1, 2))),
        "x_dec": noise(part_splits[1], (REQS, 2, D), 1.0, 6.0, ((0, 8), (2, 2))),
        "q_dec": draw_q_dec(jax.random.fold_in(jax.random.fold_in(splits[12], part), 71), part),
        "kv_weight": noise(splits[3], (D, KVW), D ** -0.5, 0.0625, ((0, 2),)),
        "kv_gain": jnp.clip(1.0 + 0.18 * jax.random.normal(splits[4], (LAT,), jnp.float32), 0.1, 1.9),
        "up_key": noise(splits[5], (HEADS, NOPE, LAT), NOPE ** -0.5, 0.5, ((0, 2),)),
        "up_value": noise(splits[6], (HEADS, LAT, VDIM), LAT ** -0.5, 0.25, ((0, 2),)),
        "out_weight": noise(splits[7], (HEADS * VDIM, D), (HEADS * VDIM) ** -0.5, 0.046875, ((0, 2), (1, 8))),
        "old_cache": draw_old_cache(jax.random.fold_in(jax.random.fold_in(splits[12], part), 71), part),
        "old_lens": uneven_parts(part_splits[9], OLD_REQS, CL * OLD_REQS // 2, CL, 2).astype(jnp.int32),
        "prompt_lens": jax.vmap(lambda own: uneven_parts(own, NEW_DEV, PTOK, PMAX, 2))(jax.random.split(part_splits[10], NEW_DEV)).reshape((NEW_DEV, NEW_DEV)).astype(jnp.int32),
        "owners": jax.vmap(lambda own: jax.random.permutation(own, NEW_DEV))(jax.random.split(part_splits[11], NEW_DEV)).reshape((NEW_DEV, NEW_DEV)).astype(jnp.int32),
    }


def normalize(raw_rows, kv_gain):
    latent = raw_rows[..., :LAT]
    factor = lax.rsqrt(lax.optimization_barrier(jnp.mean(latent * latent, axis=-1, keepdims=True)) + 1e-06)
    return jnp.concatenate([latent * factor * kv_gain, raw_rows[..., LAT:]], axis=-1).astype(jnp.bfloat16)

def attend(cache_rows, lengths, queries, own_keys, up_value, scaling):
    query_f = queries.astype(jnp.float32)
    cache_f = cache_rows.astype(jnp.float32)
    keys_f = own_keys.astype(jnp.float32)
    scores = jnp.einsum('rihc,rlc->rihl', query_f, cache_f) * scaling
    places = jnp.arange(cache_rows.shape[1], dtype=jnp.int32)
    inside = places[None, :] < lengths[:, None]
    scores = jnp.where(inside[:, None, None, :], scores, -jnp.inf)
    recent = jnp.einsum('rihc,rjc->rihj', query_f, keys_f) * scaling
    positions = jnp.arange(own_keys.shape[1], dtype=jnp.int32)
    causal = positions[:, None] >= positions[None, :]
    recent = jnp.where(causal[None, :, None, :], recent, -jnp.inf)
    highest = jnp.maximum(lax.optimization_barrier(jnp.max(scores, axis=-1)), lax.optimization_barrier(jnp.max(recent, axis=-1)))[..., None]
    far_terms = jnp.exp(scores - highest)
    near_terms = jnp.exp(recent - highest)
    totals = lax.optimization_barrier(jnp.sum(far_terms, axis=-1, keepdims=True)) + lax.optimization_barrier(jnp.sum(near_terms, axis=-1, keepdims=True))
    far_weights = (far_terms / totals).astype(jnp.bfloat16)
    near_weights = (near_terms / totals).astype(jnp.bfloat16)
    combined = jnp.einsum('rihl,rlc->rihc', far_weights.astype(jnp.float32), cache_f[..., :LAT])
    combined = combined + jnp.einsum('rihj,rjc->rihc', near_weights.astype(jnp.float32), keys_f[..., :LAT])
    combined = combined.astype(jnp.bfloat16)
    per_head = jnp.einsum('rihc,hcv->rihv', combined.astype(jnp.float32), up_value.astype(jnp.float32))
    per_head = per_head.astype(jnp.bfloat16)
    return per_head.reshape(cache_rows.shape[0] * own_keys.shape[1], -1)

def reference(x_pre, x_dec, q_dec, kv_weight, kv_gain, up_key, up_value, out_weight, old_cache, old_lens, prompt_lens, owners):
    pre_rows = normalize(jnp.dot(x_pre, kv_weight, preferred_element_type=jnp.float32), kv_gain)
    dec_raw = jnp.dot(x_dec.reshape(REQS * 2, D), kv_weight, preferred_element_type=jnp.float32)
    dec_keys = normalize(dec_raw, kv_gain).reshape(REQS, 2, KVW)
    begins = (jnp.cumsum(prompt_lens, axis=1) - prompt_lens).astype(jnp.int32)
    targets = jnp.arange(NEW_DEV, dtype=jnp.int32)
    chosen = owners[:, :, None] == targets[None, None, :]
    source_start = lax.optimization_barrier(jnp.sum(jnp.where(chosen, begins[:, :, None], 0), axis=1)).astype(jnp.int32)
    source_len = lax.optimization_barrier(jnp.sum(jnp.where(chosen, prompt_lens[:, :, None], 0), axis=1)).astype(jnp.int32)
    queries_all = q_dec.reshape(REQS, 2, HEADS, QK)
    scaling = 1.0 / math.sqrt(QK)
    sources = jnp.arange(NEW_DEV, dtype=jnp.int32)
    offsets = jnp.arange(PMAX, dtype=jnp.int32)

    def one_owner(owner):
        begin_rows = source_start[:, owner]
        counts = source_len[:, owner]
        positions = sources[:, None] * PTOK + begin_rows[:, None] + offsets[None, :]
        positions = jnp.clip(positions, 0, PROMPT_ROWS - 1).astype(jnp.int32)
        picked = jnp.take(pre_rows, positions, axis=0)
        keep_mask = (offsets[None, :] < counts[:, None])[:, :, None]
        new_cache = jnp.where(keep_mask, picked, jnp.zeros_like(picked))
        first_req = (owner * REQ_DEV).astype(jnp.int32)
        query_block = lax.dynamic_slice_in_dim(queries_all, first_req, REQ_DEV, 0)
        key_block = lax.dynamic_slice_in_dim(dec_keys, first_req, REQ_DEV, 0)
        first_old = (owner * R_OLD).astype(jnp.int32)
        cache_block = lax.dynamic_slice_in_dim(old_cache, first_old, R_OLD, 0)
        length_block = lax.dynamic_slice_in_dim(old_lens, first_old, R_OLD, 0)
        absorbed = jnp.einsum('rihn,hnc->rihc', query_block[..., :NOPE].astype(jnp.float32), up_key.astype(jnp.float32))
        absorbed = absorbed.astype(jnp.bfloat16)
        full_query = jnp.concatenate([absorbed, query_block[..., NOPE:]], axis=-1)
        fresh = attend(new_cache, counts, full_query[:NEW_DEV], key_block[:NEW_DEV], up_value, scaling)
        earlier = attend(cache_block, length_block, full_query[NEW_DEV:], key_block[NEW_DEV:], up_value, scaling)
        return jnp.concatenate([fresh, earlier], axis=0)
    head_rows = lax.map(one_owner, jnp.arange(NEW_DEV, dtype=jnp.int32))
    head_rows = head_rows.reshape(REQS * 2, HEADS * VDIM)
    return jnp.dot(head_rows, out_weight, preferred_element_type=jnp.float32).astype(jnp.bfloat16)
```

```python
import math

import jax
import jax.numpy as jnp
from jax import lax
from jax.sharding import PartitionSpec as P

ROPE = 64
NOPE = 128


def normalize(raw_rows, kv_gain):
    lat_width = kv_gain.shape[0]
    latent = raw_rows[..., :lat_width]
    factor = lax.rsqrt(jnp.mean(latent * latent, axis=-1, keepdims=True) + 1e-06)
    return jnp.concatenate([latent * factor * kv_gain, raw_rows[..., lat_width:]], axis=-1).astype(
        jnp.bfloat16
    )


def tp_sum(part):
    if lax.axis_size("tp") == 2:
        return part + lax.ppermute(part, "tp", [(0, 1), (1, 0)])
    return lax.psum(part, "tp")


def tp_scatter(part):
    if lax.axis_size("tp") == 2:
        half = part.shape[0] // 2
        me = lax.axis_index("tp")
        mine = lax.dynamic_slice_in_dim(part, me * half, half, 0)
        other = lax.dynamic_slice_in_dim(part, (1 - me) * half, half, 0)
        return mine + lax.ppermute(other, "tp", [(0, 1), (1, 0)])
    return lax.psum_scatter(part, "tp", scatter_dimension=0, tiled=True)


def attend(cache, inside, queries, own_keys, lat_width, scaling):
    scores = jnp.einsum("bgihc,blc->bgihl", queries, cache, preferred_element_type=jnp.float32)
    scores = jnp.where(inside[:, :, None, None, :], scores * scaling, -jnp.inf)
    recent = (
        jnp.einsum("bgihc,bgjc->bgihj", queries, own_keys, preferred_element_type=jnp.float32)
        * scaling
    )
    positions = jnp.arange(own_keys.shape[2], dtype=jnp.int32)
    causal = positions[:, None] >= positions[None, :]
    recent = jnp.where(causal[:, None, :], recent, -jnp.inf)
    highest = jnp.maximum(jnp.max(scores, axis=-1), jnp.max(recent, axis=-1))[..., None]
    far = jnp.exp(scores - highest)
    near = jnp.exp(recent - highest)
    totals = jnp.sum(far, axis=-1, keepdims=True) + jnp.sum(near, axis=-1, keepdims=True)
    combined = jnp.einsum(
        "bgihl,blc->bgihc",
        far.astype(jnp.bfloat16),
        cache[..., :lat_width],
        preferred_element_type=jnp.float32,
    )
    keys = own_keys[..., :lat_width].astype(jnp.float32)
    for j in range(own_keys.shape[2]):
        combined = combined + near[..., j : j + 1] * keys[:, :, j][:, :, None, None, :]
    return (combined / totals).astype(jnp.bfloat16)


def body(
    x_pre,
    x_dec,
    q_dec,
    kv_weight,
    kv_gain,
    up_key,
    up_value,
    out_weight,
    old_cache,
    old_lens,
    prompt_lens,
    owners,
):
    pool_size = lax.axis_size("pool")
    own_pool = lax.axis_index("pool")
    requests = x_dec.shape[0]
    model_part = x_pre.shape[1]
    heads_here = up_key.shape[0]
    lat_width = kv_gain.shape[0]
    scaling = 1.0 / math.sqrt(NOPE + ROPE)

    fresh_q = lax.all_to_all(q_dec[:pool_size], "pool", split_axis=0, concat_axis=0, tiled=True)
    fresh_x = lax.all_to_all(x_dec[:pool_size], "pool", split_axis=0, concat_axis=0, tiled=True)

    chunks = 4
    rows = x_pre.shape[0] // chunks
    pre_rows = jnp.concatenate(
        [
            normalize(
                tp_sum(
                    jnp.dot(
                        x_pre[c * rows : (c + 1) * rows],
                        kv_weight,
                        preferred_element_type=jnp.float32,
                    )
                ),
                kv_gain,
            )
            for c in range(chunks)
        ],
        axis=0,
    )
    x_rows = jnp.concatenate([fresh_x, x_dec[pool_size:]], axis=0).reshape(-1, model_part)
    dec_raw = tp_sum(jnp.dot(x_rows, kv_weight, preferred_element_type=jnp.float32))
    dec_keys = normalize(dec_raw, kv_gain).reshape(requests, 2, -1)

    my_lengths = lax.dynamic_index_in_dim(prompt_lens, own_pool, 0, keepdims=False)
    my_owners = lax.dynamic_index_in_dim(owners, own_pool, 0, keepdims=False)
    targets = jnp.arange(pool_size, dtype=jnp.int32)
    chosen = my_owners[:, None] == targets[None, :]
    begins = jnp.cumsum(my_lengths) - my_lengths
    start = jnp.sum(jnp.where(chosen, begins[:, None], 0), axis=0)
    count = jnp.sum(jnp.where(chosen, my_lengths[:, None], 0), axis=0)
    places = jnp.arange(x_pre.shape[0], dtype=jnp.int32)
    fresh_inside = (places[None] >= start[:, None]) & (places[None] < (start + count)[:, None])
    old_inside = jnp.arange(old_cache.shape[1], dtype=jnp.int32)[None] < old_lens[:, None]

    q_rows = jnp.concatenate([fresh_q, q_dec[pool_size:]], axis=0).reshape(
        requests, 2, heads_here, NOPE + ROPE
    )
    absorbed = jnp.einsum(
        "rihn,hnc->rihc", q_rows[..., :NOPE], up_key, preferred_element_type=jnp.float32
    )
    full_query = jnp.concatenate([absorbed.astype(jnp.bfloat16), q_rows[..., NOPE:]], axis=-1)
    earlier = attend(
        old_cache,
        old_inside[:, None],
        full_query[pool_size:, None],
        dec_keys[pool_size:, None],
        lat_width,
        scaling,
    )[:, 0]
    fresh = attend(
        pre_rows[None],
        fresh_inside[None],
        full_query[None, :pool_size],
        dec_keys[None, :pool_size],
        lat_width,
        scaling,
    )[0]
    combined = jnp.concatenate([fresh, earlier], axis=0)
    head_rows = (
        jnp.einsum("rihc,hcv->rihv", combined, up_value, preferred_element_type=jnp.float32)
        .astype(jnp.bfloat16)
        .reshape(requests * 2, -1)
    )
    gathered = lax.all_gather(head_rows, "pool", axis=0, tiled=True)
    partial_out = jnp.dot(gathered, out_weight, preferred_element_type=jnp.float32)
    cols = partial_out.shape[-1]
    partial_out = partial_out.reshape(pool_size, requests, 2, cols)
    partial_out = jnp.concatenate(
        [partial_out[:, :pool_size].transpose(1, 0, 2, 3), partial_out[:, pool_size:]], axis=1
    ).reshape(-1, cols)
    return tp_scatter(partial_out).astype(jnp.bfloat16)


def solution(mesh):
    placed = (
        P(("groups", "pool"), "tp"),
        P(("groups", "pool"), None, "tp"),
        P(("groups", "pool"), None, "tp"),
        P("tp", None),
        P(),
        P("tp", None, None),
        P("tp", None, None),
        P("tp", "pool"),
        P(("groups", "pool"), None, None),
        P(("groups", "pool")),
        P("groups", None),
        P("groups", None),
    )
    return jax.shard_map(
        body, mesh=mesh, in_specs=placed, out_specs=P(("groups", "tp"), "pool"), check_vma=False
    )
```

```python
import math

import jax
import jax.numpy as jnp
from jax import lax
from jax.experimental import pallas as pl
from jax.experimental.pallas import tpu as pltpu
from jax.sharding import PartitionSpec as P

ROPE = 64
NOPE = 128


def normalize(raw_rows, kv_gain):
    lat_width = kv_gain.shape[0]
    latent = raw_rows[..., :lat_width]
    factor = lax.rsqrt(jnp.mean(latent * latent, axis=-1, keepdims=True) + 1e-06)
    return jnp.concatenate([latent * factor * kv_gain, raw_rows[..., lat_width:]], axis=-1).astype(
        jnp.bfloat16
    )


def tp_sum(part):
    if lax.axis_size("tp") == 2:
        return part + lax.ppermute(part, "tp", [(0, 1), (1, 0)])
    return lax.psum(part, "tp")


def tp_scatter(part):
    if lax.axis_size("tp") == 2:
        half = part.shape[0] // 2
        me = lax.axis_index("tp")
        mine = lax.dynamic_slice_in_dim(part, me * half, half, 0)
        other = lax.dynamic_slice_in_dim(part, (1 - me) * half, half, 0)
        return mine + lax.ppermute(other, "tp", [(0, 1), (1, 0)])
    return lax.psum_scatter(part, "tp", scatter_dimension=0, tiled=True)


def attend(cache, inside, queries, own_keys, lat_width, scaling):
    scores = jnp.einsum("bgihc,blc->bgihl", queries, cache, preferred_element_type=jnp.float32)
    scores = jnp.where(inside[:, :, None, None, :], scores * scaling, -jnp.inf)
    recent = (
        jnp.einsum("bgihc,bgjc->bgihj", queries, own_keys, preferred_element_type=jnp.float32)
        * scaling
    )
    positions = jnp.arange(own_keys.shape[2], dtype=jnp.int32)
    causal = positions[:, None] >= positions[None, :]
    recent = jnp.where(causal[:, None, :], recent, -jnp.inf)
    highest = jnp.maximum(jnp.max(scores, axis=-1), jnp.max(recent, axis=-1))[..., None]
    far = jnp.exp(scores - highest)
    near = jnp.exp(recent - highest)
    totals = jnp.sum(far, axis=-1, keepdims=True) + jnp.sum(near, axis=-1, keepdims=True)
    combined = jnp.einsum(
        "bgihl,blc->bgihc",
        far.astype(jnp.bfloat16),
        cache[..., :lat_width],
        preferred_element_type=jnp.float32,
    )
    keys = own_keys[..., :lat_width].astype(jnp.float32)
    for j in range(own_keys.shape[2]):
        combined = combined + near[..., j : j + 1] * keys[:, :, j][:, :, None, None, :]
    return (combined / totals).astype(jnp.bfloat16)


WIDE = 2


def gather_out_kernel(
    high,
    h_ref,
    w_hbm,
    fresh_ref,
    old_ref,
    blocks,
    weight,
    total,
    land_fresh,
    land_old,
    recv_sem,
    send_sem,
    local_sem,
    pair_send,
    pair_recv,
):
    me = lax.axis_index("pool")
    core = lax.axis_index("tp")
    row = lax.div(me, WIDE)
    col = lax.rem(me, WIDE)
    side = row * WIDE + (1 - col)
    up, down = me + WIDE, me - WIDE
    has_up, has_down = row < high - 1, row > 0
    w_copy = pltpu.make_async_copy(w_hbm, weight, local_sem.at[0])
    w_copy.start()

    barrier = pltpu.get_barrier_semaphore()

    def greet(target):
        pl.semaphore_signal(
            barrier, inc=1, device_id=target, device_id_type=pl.DeviceIdType.MESH
        )

    greet({"pool": side})
    greet({"tp": 1 - core})
    pl.when(has_up)(lambda: greet({"pool": up}))
    pl.when(has_down)(lambda: greet({"pool": down}))
    pl.semaphore_wait(barrier, 2 + has_up.astype(jnp.int32) + has_down.astype(jnp.int32))

    def copy(piece, slot, way, own=False):
        return pltpu.make_async_remote_copy(
            src_ref=h_ref.at[piece] if own else blocks.at[piece, slot],
            dst_ref=blocks.at[piece, slot],
            send_sem=send_sem.at[piece, slot, way],
            recv_sem=recv_sem.at[piece, slot],
            device_id={"pool": (side, up, down)[way]},
            device_id_type=pl.DeviceIdType.MESH,
        )

    for piece in range(2):
        pl.when(has_up)(lambda: copy(piece, me, 1, True).start())
        pl.when(has_down)(lambda: copy(piece, me, 2, True).start())
        copy(piece, me, 0, True).start()
        pltpu.make_async_copy(h_ref.at[piece], blocks.at[piece, me], local_sem.at[1 + piece]).start()

    for step in range(1, high):
        for piece in range(2):

            @pl.when(row >= step)
            def _():
                slot = me - step * WIDE
                copy(piece, slot, 0).wait_recv()
                pl.when(has_up)(lambda: copy(piece, slot, 1).start())
                copy(piece, slot, 0).start()

            @pl.when(row + step < high)
            def _():
                slot = me + step * WIDE
                copy(piece, slot, 0).wait_recv()
                pl.when(has_down)(lambda: copy(piece, slot, 2).start())
                copy(piece, slot, 0).start()

    for piece in range(2):
        for at in range(high):
            copy(piece, at * WIDE + 1 - col, 0).wait_recv()
        pltpu.make_async_copy(
            h_ref.at[piece], blocks.at[piece, me], local_sem.at[1 + piece]
        ).wait()
    w_copy.wait()

    total[...] = jnp.zeros_like(total)
    depth = 1024
    slots, rows = blocks.shape[1:3]

    @pl.loop(0, weight.shape[0] // depth)
    def _(k):
        cut = pl.ds(pl.multiple_of(k * depth, depth), depth)
        left = blocks[:, :, :, cut].reshape(2 * slots * rows, depth)
        total[...] += jnp.dot(
            left, weight[cut, :], preferred_element_type=jnp.float32
        ).reshape(total.shape)

    half_rows, half_slots = rows // 2, slots // 2
    their_rows = pl.ds(pl.multiple_of((1 - core) * half_rows, half_rows), half_rows)
    my_rows = pl.ds(pl.multiple_of(core * half_rows, half_rows), half_rows)
    pair = [
        pltpu.make_async_remote_copy(
            src_ref=src,
            dst_ref=dst,
            send_sem=pair_send.at[n],
            recv_sem=pair_recv.at[n],
            device_id={"tp": 1 - core},
            device_id_type=pl.DeviceIdType.MESH,
        )
        for n, (src, dst) in enumerate(
            (
                (total.at[0, :, their_rows, :], land_fresh),
                (total.at[1, pl.ds((1 - core) * half_slots, half_slots)], land_old),
            )
        )
    ]
    for one in pair:
        one.start()
    pair[0].wait()
    fresh_ref[...] = (total[0, :, my_rows, :] + land_fresh[...]).astype(fresh_ref.dtype)
    pair[1].wait()
    old_ref[...] = (total[1, pl.ds(core * half_slots, half_slots)] + land_old[...]).astype(
        old_ref.dtype
    )

    for piece in range(2):
        copy(piece, me, 0, True).wait_send()
        pl.when(has_up)(lambda: copy(piece, me, 1, True).wait_send())
        pl.when(has_down)(lambda: copy(piece, me, 2, True).wait_send())
    for step in range(1, high):
        for piece in range(2):

            @pl.when(row >= step)
            def _():
                slot = me - step * WIDE
                pl.when(has_up)(lambda: copy(piece, slot, 1).wait_send())
                copy(piece, slot, 0).wait_send()

            @pl.when(row + step < high)
            def _():
                slot = me + step * WIDE
                pl.when(has_down)(lambda: copy(piece, slot, 2).wait_send())
                copy(piece, slot, 0).wait_send()


def gather_out(fresh_rows, old_rows, out_weight):
    pool = lax.axis_size("pool")
    rows = 2 * pool
    n_old = old_rows.shape[0]
    depth, cols = out_weight.shape
    old_rows = jnp.pad(old_rows, ((0, rows - n_old), (0, 0)))
    fresh, old = pl.pallas_call(
        lambda *refs: gather_out_kernel(pool // WIDE, *refs),
        out_shape=(
            jax.ShapeDtypeStruct((pool, rows // 2, cols), jnp.float32),
            jax.ShapeDtypeStruct((pool // 2, rows, cols), jnp.float32),
        ),
        in_specs=[
            pl.BlockSpec(memory_space=pltpu.VMEM),
            pl.BlockSpec(memory_space=pl.ANY),
        ],
        out_specs=[pl.BlockSpec(memory_space=pltpu.VMEM)] * 2,
        scratch_shapes=[
            pltpu.VMEM((2, pool, rows, depth), jnp.bfloat16),
            pltpu.VMEM((depth, cols), jnp.bfloat16),
            pltpu.VMEM((2, pool, rows, cols), jnp.float32),
            pltpu.VMEM((pool, rows // 2, cols), jnp.float32),
            pltpu.VMEM((pool // 2, rows, cols), jnp.float32),
            pltpu.SemaphoreType.DMA((2, pool)),
            pltpu.SemaphoreType.DMA((2, pool, 3)),
            pltpu.SemaphoreType.DMA((3,)),
            pltpu.SemaphoreType.DMA((2,)),
            pltpu.SemaphoreType.DMA((2,)),
        ],
        compiler_params=pltpu.CompilerParams(
            collective_id=0, has_side_effects=True, vmem_limit_bytes=40 * 2**20
        ),
    )(jnp.stack([fresh_rows, old_rows]), out_weight)
    fresh = fresh.reshape(pool, pool // 2, 2, cols).transpose(1, 0, 2, 3)
    old = old[:, :n_old].reshape(pool // 2, n_old // 2, 2, cols)
    return jnp.concatenate([fresh, old], axis=1).reshape(-1, cols).astype(jnp.bfloat16)


def body(
    x_pre,
    x_dec,
    q_dec,
    kv_weight,
    kv_gain,
    up_key,
    up_value,
    out_weight,
    old_cache,
    old_lens,
    prompt_lens,
    owners,
):
    pool_size = lax.axis_size("pool")
    own_pool = lax.axis_index("pool")
    requests = x_dec.shape[0]
    model_part = x_pre.shape[1]
    heads_here = up_key.shape[0]
    lat_width = kv_gain.shape[0]
    scaling = 1.0 / math.sqrt(NOPE + ROPE)

    fresh_q = lax.all_to_all(q_dec[:pool_size], "pool", split_axis=0, concat_axis=0, tiled=True)
    fresh_x = lax.all_to_all(x_dec[:pool_size], "pool", split_axis=0, concat_axis=0, tiled=True)

    chunks = 4
    rows = x_pre.shape[0] // chunks
    pre_rows = jnp.concatenate(
        [
            normalize(
                tp_sum(
                    jnp.dot(
                        x_pre[c * rows : (c + 1) * rows],
                        kv_weight,
                        preferred_element_type=jnp.float32,
                    )
                ),
                kv_gain,
            )
            for c in range(chunks)
        ],
        axis=0,
    )
    x_rows = jnp.concatenate([fresh_x, x_dec[pool_size:]], axis=0).reshape(-1, model_part)
    dec_raw = tp_sum(jnp.dot(x_rows, kv_weight, preferred_element_type=jnp.float32))
    dec_keys = normalize(dec_raw, kv_gain).reshape(requests, 2, -1)

    my_lengths = lax.dynamic_index_in_dim(prompt_lens, own_pool, 0, keepdims=False)
    my_owners = lax.dynamic_index_in_dim(owners, own_pool, 0, keepdims=False)
    targets = jnp.arange(pool_size, dtype=jnp.int32)
    chosen = my_owners[:, None] == targets[None, :]
    begins = jnp.cumsum(my_lengths) - my_lengths
    start = jnp.sum(jnp.where(chosen, begins[:, None], 0), axis=0)
    count = jnp.sum(jnp.where(chosen, my_lengths[:, None], 0), axis=0)
    places = jnp.arange(x_pre.shape[0], dtype=jnp.int32)
    fresh_inside = (places[None] >= start[:, None]) & (places[None] < (start + count)[:, None])
    old_inside = jnp.arange(old_cache.shape[1], dtype=jnp.int32)[None] < old_lens[:, None]

    q_rows = jnp.concatenate([fresh_q, q_dec[pool_size:]], axis=0).reshape(
        requests, 2, heads_here, NOPE + ROPE
    )
    absorbed = jnp.einsum(
        "rihn,hnc->rihc", q_rows[..., :NOPE], up_key, preferred_element_type=jnp.float32
    )
    full_query = jnp.concatenate([absorbed.astype(jnp.bfloat16), q_rows[..., NOPE:]], axis=-1)
    earlier = attend(
        old_cache,
        old_inside[:, None],
        full_query[pool_size:, None],
        dec_keys[pool_size:, None],
        lat_width,
        scaling,
    )[:, 0]
    fresh = attend(
        pre_rows[None],
        fresh_inside[None],
        full_query[None, :pool_size],
        dec_keys[None, :pool_size],
        lat_width,
        scaling,
    )[0]
    combined = jnp.concatenate([fresh, earlier], axis=0)
    head_rows = (
        jnp.einsum("rihc,hcv->rihv", combined, up_value, preferred_element_type=jnp.float32)
        .astype(jnp.bfloat16)
        .reshape(requests * 2, -1)
    )
    if lax.axis_size("tp") == 2 and pool_size == 8:
        return gather_out(head_rows[: 2 * pool_size], head_rows[2 * pool_size :], out_weight)
    gathered = lax.all_gather(head_rows, "pool", axis=0, tiled=True)
    partial_out = jnp.dot(gathered, out_weight, preferred_element_type=jnp.float32)
    cols = partial_out.shape[-1]
    partial_out = partial_out.reshape(pool_size, requests, 2, cols)
    partial_out = jnp.concatenate(
        [partial_out[:, :pool_size].transpose(1, 0, 2, 3), partial_out[:, pool_size:]], axis=1
    ).reshape(-1, cols)
    return tp_scatter(partial_out).astype(jnp.bfloat16)


def solution(mesh):
    placed = (
        P(("groups", "pool"), "tp"),
        P(("groups", "pool"), None, "tp"),
        P(("groups", "pool"), None, "tp"),
        P("tp", None),
        P(),
        P("tp", None, None),
        P("tp", None, None),
        P("tp", "pool"),
        P(("groups", "pool"), None, None),
        P(("groups", "pool")),
        P("groups", None),
        P("groups", None),
    )
    return jax.shard_map(
        body, mesh=mesh, in_specs=placed, out_specs=P(("groups", "tp"), "pool"), check_vma=False
    )
```

```python
import math

import jax
import jax.numpy as jnp
from jax import lax
from jax.experimental import pallas as pl
from jax.experimental.pallas import tpu as pltpu
from jax.sharding import PartitionSpec as P

ROPE = 64
NOPE = 128


def normalize(raw_rows, kv_gain):
    lat_width = kv_gain.shape[0]
    latent = raw_rows[..., :lat_width]
    factor = lax.rsqrt(jnp.mean(latent * latent, axis=-1, keepdims=True) + 1e-06)
    return jnp.concatenate([latent * factor * kv_gain, raw_rows[..., lat_width:]], axis=-1).astype(
        jnp.bfloat16
    )


def tp_sum(part):
    if lax.axis_size("tp") == 2:
        return part + lax.ppermute(part, "tp", [(0, 1), (1, 0)])
    return lax.psum(part, "tp")


def tp_scatter(part):
    if lax.axis_size("tp") == 2:
        half = part.shape[0] // 2
        me = lax.axis_index("tp")
        mine = lax.dynamic_slice_in_dim(part, me * half, half, 0)
        other = lax.dynamic_slice_in_dim(part, (1 - me) * half, half, 0)
        return mine + lax.ppermute(other, "tp", [(0, 1), (1, 0)])
    return lax.psum_scatter(part, "tp", scatter_dimension=0, tiled=True)


def attend_kernel(width, scaling, lo_ref, hi_ref, q_ref, own_ref, cache_ref, out_ref):
    at = pl.program_id(0)
    lo, hi = lo_ref[at], hi_ref[at]
    lat_width = out_ref.shape[-1]
    room = cache_ref.shape[-1] - width
    base = pl.multiple_of(jnp.minimum(lax.div(lo, 128) * 128, room), 128) if room else 0
    query = q_ref[0]
    own = own_ref[0]
    keys = cache_ref[0, :, pl.ds(base, width)]
    scores = jnp.dot(query, keys, preferred_element_type=jnp.float32) * scaling
    places = base + lax.broadcasted_iota(jnp.int32, scores.shape, 1)
    scores = jnp.where((places >= lo) & (places < hi), scores, -jnp.inf)
    flat = (((1,), (1,)), ((), ()))
    recent = lax.dot_general(query, own, flat, preferred_element_type=jnp.float32) * scaling
    later = lax.broadcasted_iota(jnp.int32, recent.shape, 1)
    second = lax.broadcasted_iota(jnp.int32, recent.shape, 0) >= recent.shape[0] // 2
    recent = jnp.where(later <= second.astype(jnp.int32), recent, -jnp.inf)
    highest = jnp.maximum(
        jnp.max(scores, axis=1, keepdims=True), jnp.max(recent, axis=1, keepdims=True)
    )
    far = jnp.exp(scores - highest)
    near = jnp.exp(recent - highest)
    inverse = 1.0 / (jnp.sum(far, axis=1, keepdims=True) + jnp.sum(near, axis=1, keepdims=True))
    combined = lax.dot_general(
        (far * inverse).astype(jnp.bfloat16),
        keys[:lat_width],
        flat,
        preferred_element_type=jnp.float32,
    ) + jnp.dot(
        (near * inverse).astype(jnp.bfloat16),
        own[:, :lat_width],
        preferred_element_type=jnp.float32,
    )
    out_ref[0] = combined.astype(out_ref.dtype)


def attend(cache, lo, hi, queries, own_keys, lat_width, width, scaling):
    number, steps, heads, wide = queries.shape
    shared = cache.shape[0] == 1
    own_keys = jnp.pad(own_keys, ((0, 0), (0, 16 - steps), (0, 0)))
    out = pl.pallas_call(
        lambda *refs: attend_kernel(width, scaling, *refs),
        grid_spec=pltpu.PrefetchScalarGridSpec(
            num_scalar_prefetch=2,
            grid=(number,),
            in_specs=[
                pl.BlockSpec((1, steps * heads, wide), lambda r, lo, hi: (r, 0, 0)),
                pl.BlockSpec((1, 16, wide), lambda r, lo, hi: (r, 0, 0)),
                pl.BlockSpec(
                    (1,) + cache.shape[1:], lambda r, lo, hi: (0 if shared else r, 0, 0)
                ),
            ],
            out_specs=pl.BlockSpec((1, steps * heads, lat_width), lambda r, lo, hi: (r, 0, 0)),
        ),
        out_shape=jax.ShapeDtypeStruct((number, steps * heads, lat_width), jnp.bfloat16),
        compiler_params=pltpu.CompilerParams(vmem_limit_bytes=24 * 2**20),
        cost_estimate=pl.CostEstimate(
            flops=4 * number * steps * heads * wide * width,
            bytes_accessed=2 * (cache.size + 2 * queries.size),
            transcendentals=number * steps * heads * width,
        ),
    )(lo, hi, queries.reshape(number, steps * heads, wide), own_keys, cache)
    return out.reshape(number, steps, heads, lat_width)


WIDE = 2


def gather_out_kernel(
    high,
    h_ref,
    old_hbm,
    w_hbm,
    fresh_ref,
    old_ref,
    blocks,
    old_rows,
    weight,
    total,
    land_fresh,
    land_old,
    recv_sem,
    send_sem,
    local_sem,
    pair_send,
    pair_recv,
):
    me = lax.axis_index("pool")
    core = lax.axis_index("tp")
    row = lax.div(me, WIDE)
    col = lax.rem(me, WIDE)
    side = row * WIDE + (1 - col)
    up, down = me + WIDE, me - WIDE
    has_up, has_down = row < high - 1, row > 0
    w_copy = pltpu.make_async_copy(w_hbm, weight, local_sem.at[0])
    w_copy.start()
    old_copy = pltpu.make_async_copy(old_hbm, old_rows, local_sem.at[1])
    old_copy.start()
    own_copy = pltpu.make_async_copy(h_ref, blocks.at[me], local_sem.at[2])

    barrier = pltpu.get_barrier_semaphore()

    def greet(target):
        pl.semaphore_signal(
            barrier, inc=1, device_id=target, device_id_type=pl.DeviceIdType.MESH
        )

    greet({"pool": side})
    greet({"tp": 1 - core})
    pl.when(has_up)(lambda: greet({"pool": up}))
    pl.when(has_down)(lambda: greet({"pool": down}))
    pl.semaphore_wait(barrier, 2 + has_up.astype(jnp.int32) + has_down.astype(jnp.int32))

    def copy(slot, way, own=False):
        return pltpu.make_async_remote_copy(
            src_ref=h_ref if own else blocks.at[slot],
            dst_ref=blocks.at[slot],
            send_sem=send_sem.at[slot, way],
            recv_sem=recv_sem.at[slot],
            device_id={"pool": (side, up, down)[way]},
            device_id_type=pl.DeviceIdType.MESH,
        )

    def pair_copy(n, src, dst):
        return pltpu.make_async_remote_copy(
            src_ref=src,
            dst_ref=dst,
            send_sem=pair_send.at[n],
            recv_sem=pair_recv.at[n],
            device_id={"tp": 1 - core},
            device_id_type=pl.DeviceIdType.MESH,
        )

    pl.when(has_up)(lambda: copy(me, 1, True).start())
    pl.when(has_down)(lambda: copy(me, 2, True).start())
    copy(me, 0, True).start()
    own_copy.start()
    total[...] = jnp.zeros_like(total)
    slots, rows, depth = blocks.shape
    part = depth // 8
    half_rows, half_slots = rows // 2, slots // 2
    w_copy.wait()
    old_copy.wait()

    def multiply(piece, source, first, last):
        @pl.loop(first, last)
        def _(k):
            cut = pl.ds(pl.multiple_of(k * part, part), part)
            left = source[:, :, cut].reshape(slots * rows, part)
            total[piece] += jnp.dot(
                left, weight[cut, :], preferred_element_type=jnp.float32
            ).reshape(total.shape[1:])

    bounds = [8 * n // high for n in range(high + 1)]
    for step in range(1, high):
        multiply(1, old_rows, bounds[step - 1], bounds[step])

        @pl.when(row >= step)
        def _():
            slot = me - step * WIDE
            copy(slot, 0).wait_recv()
            pl.when(has_up)(lambda: copy(slot, 1).start())
            copy(slot, 0).start()

        @pl.when(row + step < high)
        def _():
            slot = me + step * WIDE
            copy(slot, 0).wait_recv()
            pl.when(has_down)(lambda: copy(slot, 2).start())
            copy(slot, 0).start()

    multiply(1, old_rows, bounds[high - 1], 8)
    old_pair = pair_copy(1, total.at[1, pl.ds((1 - core) * half_slots, half_slots)], land_old)
    old_pair.start()
    own_copy.wait()
    for at in range(high):
        copy(at * WIDE + 1 - col, 0).wait_recv()
    multiply(0, blocks, 0, 8)
    their_rows = pl.ds(pl.multiple_of((1 - core) * half_rows, half_rows), half_rows)
    my_rows = pl.ds(pl.multiple_of(core * half_rows, half_rows), half_rows)
    fresh_pair = pair_copy(0, total.at[0, :, their_rows, :], land_fresh)
    fresh_pair.start()
    old_pair.wait()
    old_ref[...] = (total[1, pl.ds(core * half_slots, half_slots)] + land_old[...]).astype(
        old_ref.dtype
    )
    fresh_pair.wait()
    fresh_ref[...] = (total[0, :, my_rows, :] + land_fresh[...]).astype(fresh_ref.dtype)

    copy(me, 0, True).wait_send()
    pl.when(has_up)(lambda: copy(me, 1, True).wait_send())
    pl.when(has_down)(lambda: copy(me, 2, True).wait_send())
    for step in range(1, high):

        @pl.when(row >= step)
        def _():
            slot = me - step * WIDE
            pl.when(has_up)(lambda: copy(slot, 1).wait_send())
            copy(slot, 0).wait_send()

        @pl.when(row + step < high)
        def _():
            slot = me + step * WIDE
            pl.when(has_down)(lambda: copy(slot, 2).wait_send())
            copy(slot, 0).wait_send()


def gather_out(fresh_rows, old_rows, n_old, out_weight):
    pool = lax.axis_size("pool")
    rows = 2 * pool
    depth, cols = out_weight.shape
    fresh, old = pl.pallas_call(
        lambda *refs: gather_out_kernel(pool // WIDE, *refs),
        out_shape=(
            jax.ShapeDtypeStruct((pool, rows // 2, cols), jnp.float32),
            jax.ShapeDtypeStruct((pool // 2, rows, cols), jnp.float32),
        ),
        in_specs=[
            pl.BlockSpec(memory_space=pltpu.VMEM),
            pl.BlockSpec(memory_space=pl.ANY),
            pl.BlockSpec(memory_space=pl.ANY),
        ],
        out_specs=[pl.BlockSpec(memory_space=pltpu.VMEM)] * 2,
        scratch_shapes=[
            pltpu.VMEM((pool, rows, depth), jnp.bfloat16),
            pltpu.VMEM((pool, rows, depth), jnp.bfloat16),
            pltpu.VMEM((depth, cols), jnp.bfloat16),
            pltpu.VMEM((2, pool, rows, cols), jnp.float32),
            pltpu.VMEM((pool, rows // 2, cols), jnp.float32),
            pltpu.VMEM((pool // 2, rows, cols), jnp.float32),
            pltpu.SemaphoreType.DMA((pool,)),
            pltpu.SemaphoreType.DMA((pool, 3)),
            pltpu.SemaphoreType.DMA((3,)),
            pltpu.SemaphoreType.DMA((2,)),
            pltpu.SemaphoreType.DMA((2,)),
        ],
        compiler_params=pltpu.CompilerParams(
            collective_id=0, has_side_effects=True, vmem_limit_bytes=40 * 2**20
        ),
    )(fresh_rows, old_rows, out_weight)
    fresh = fresh.reshape(pool, pool // 2, 2, cols).transpose(1, 0, 2, 3)
    old = old[:, :n_old].reshape(pool // 2, n_old // 2, 2, cols)
    return jnp.concatenate([fresh, old], axis=1).reshape(-1, cols).astype(jnp.bfloat16)


def body(
    x_pre,
    x_dec,
    q_dec,
    kv_weight,
    kv_gain,
    up_key,
    up_value,
    out_weight,
    old_cache,
    old_lens,
    prompt_lens,
    owners,
):
    pool_size = lax.axis_size("pool")
    own_pool = lax.axis_index("pool")
    requests = x_dec.shape[0]
    model_part = x_pre.shape[1]
    heads_here = up_key.shape[0]
    lat_width = kv_gain.shape[0]
    scaling = 1.0 / math.sqrt(NOPE + ROPE)

    query_cols = q_dec.shape[-1]
    sent = jnp.concatenate([q_dec[:pool_size], x_dec[:pool_size]], axis=-1)
    arrived = lax.all_to_all(sent, "pool", split_axis=0, concat_axis=0, tiled=True)
    fresh_q, fresh_x = arrived[..., :query_cols], arrived[..., query_cols:]

    x_rows = jnp.concatenate([fresh_x, x_dec[pool_size:]], axis=0).reshape(-1, model_part)
    dec_raw = tp_sum(jnp.dot(x_rows, kv_weight, preferred_element_type=jnp.float32))
    dec_keys = normalize(dec_raw, kv_gain).reshape(requests, 2, -1)
    q_rows = jnp.concatenate([fresh_q, q_dec[pool_size:]], axis=0).reshape(
        requests, 2, heads_here, NOPE + ROPE
    )
    absorbed = jnp.einsum(
        "rihn,hnc->rihc", q_rows[..., :NOPE], up_key, preferred_element_type=jnp.float32
    )
    full_query = jnp.concatenate([absorbed.astype(jnp.bfloat16), q_rows[..., NOPE:]], axis=-1)

    def lift(combined):
        return (
            jnp.einsum("rihc,hcv->rihv", combined, up_value, preferred_element_type=jnp.float32)
            .astype(jnp.bfloat16)
            .reshape(combined.shape[0] * 2, -1)
        )

    old_rows = lift(
        attend(
            old_cache.transpose(0, 2, 1),
            jnp.zeros_like(old_lens),
            old_lens,
            full_query[pool_size:],
            dec_keys[pool_size:],
            lat_width,
            old_cache.shape[1],
            scaling,
        )
    )
    n_old = old_rows.shape[0]
    old_rows = jnp.pad(old_rows, ((0, 2 * pool_size - n_old), (0, 0)))
    all_old = lax.all_gather(old_rows, "pool", axis=0, tiled=False)

    chunks = 4
    rows = x_pre.shape[0] // chunks
    late_weight, _ = lax.optimization_barrier((kv_weight, old_rows))
    pre_rows = jnp.concatenate(
        [
            normalize(
                tp_sum(
                    jnp.dot(
                        x_pre[c * rows : (c + 1) * rows],
                        late_weight if c else kv_weight,
                        preferred_element_type=jnp.float32,
                    )
                ),
                kv_gain,
            )
            for c in range(chunks)
        ],
        axis=0,
    )

    my_lengths = lax.dynamic_index_in_dim(prompt_lens, own_pool, 0, keepdims=False)
    my_owners = lax.dynamic_index_in_dim(owners, own_pool, 0, keepdims=False)
    targets = jnp.arange(pool_size, dtype=jnp.int32)
    chosen = my_owners[:, None] == targets[None, :]
    begins = jnp.cumsum(my_lengths) - my_lengths
    start = jnp.sum(jnp.where(chosen, begins[:, None], 0), axis=0)
    count = jnp.sum(jnp.where(chosen, my_lengths[:, None], 0), axis=0)
    longest = 2 * x_pre.shape[0] // pool_size
    window = min(-(-longest // 128) * 128 + 128, x_pre.shape[0])
    fresh_rows = lift(
        attend(
            pre_rows.T[None],
            start,
            start + count,
            full_query[:pool_size],
            dec_keys[:pool_size],
            lat_width,
            window,
            scaling,
        )
    )
    if lax.axis_size("tp") == 2 and pool_size == 8:
        return gather_out(fresh_rows, all_old, n_old, out_weight)
    all_fresh = lax.all_gather(fresh_rows, "pool", axis=0, tiled=False)
    partial_out = jnp.dot(
        jnp.concatenate([all_fresh, all_old], axis=1), out_weight, preferred_element_type=jnp.float32
    )
    cols = partial_out.shape[-1]
    partial_out = partial_out.reshape(pool_size, 2 * pool_size, 2, cols)
    partial_out = jnp.concatenate(
        [
            partial_out[:, :pool_size].transpose(1, 0, 2, 3),
            partial_out[:, pool_size : pool_size + n_old // 2],
        ],
        axis=1,
    ).reshape(-1, cols)
    return tp_scatter(partial_out).astype(jnp.bfloat16)


def solution(mesh):
    placed = (
        P(("groups", "pool"), "tp"),
        P(("groups", "pool"), None, "tp"),
        P(("groups", "pool"), None, "tp"),
        P("tp", None),
        P(),
        P("tp", None, None),
        P("tp", None, None),
        P("tp", "pool"),
        P(("groups", "pool"), None, None),
        P(("groups", "pool")),
        P("groups", None),
        P("groups", None),
    )
    return jax.shard_map(
        body, mesh=mesh, in_specs=placed, out_specs=P(("groups", "tp"), "pool"), check_vma=False
    )
```

```python
import math

import jax
import jax.numpy as jnp
from jax import lax
from jax.experimental import pallas as pl
from jax.experimental.pallas import tpu as pltpu
from jax.sharding import PartitionSpec as P

ROPE = 64
NOPE = 128


def normalize(raw_rows, kv_gain):
    lat_width = kv_gain.shape[0]
    rest = raw_rows.shape[-1] - lat_width
    latent = raw_rows[..., :lat_width]
    factor = lax.rsqrt(jnp.mean(latent * latent, axis=-1, keepdims=True) + 1e-06)
    inside = jnp.arange(raw_rows.shape[-1]) < lat_width
    gain = jnp.concatenate([kv_gain, jnp.ones((rest,), kv_gain.dtype)])
    return (raw_rows * jnp.where(inside, factor, 1.0) * gain).astype(jnp.bfloat16)


def tp_sum(part):
    if lax.axis_size("tp") == 2:
        return part + lax.ppermute(part, "tp", [(0, 1), (1, 0)])
    return lax.psum(part, "tp")


def tp_scatter(part):
    if lax.axis_size("tp") == 2:
        half = part.shape[0] // 2
        me = lax.axis_index("tp")
        mine = lax.dynamic_slice_in_dim(part, me * half, half, 0)
        other = lax.dynamic_slice_in_dim(part, (1 - me) * half, half, 0)
        return mine + lax.ppermute(other, "tp", [(0, 1), (1, 0)])
    return lax.psum_scatter(part, "tp", scatter_dimension=0, tiled=True)


def attend_kernel(width, scaling, lo_ref, hi_ref, q_ref, own_ref, cache_ref, out_ref):
    at = pl.program_id(0)
    lo, hi = lo_ref[at], hi_ref[at]
    lat_width = out_ref.shape[-1]
    room = cache_ref.shape[-1] - width
    base = pl.multiple_of(jnp.minimum(lax.div(lo, 128) * 128, room), 128) if room else 0
    query = q_ref[0]
    own = own_ref[0]
    keys = cache_ref[0, :, pl.ds(base, width)]
    scores = jnp.dot(query, keys, preferred_element_type=jnp.float32) * scaling
    places = base + lax.broadcasted_iota(jnp.int32, scores.shape, 1)
    scores = jnp.where((places >= lo) & (places < hi), scores, -jnp.inf)
    flat = (((1,), (1,)), ((), ()))
    recent = lax.dot_general(query, own, flat, preferred_element_type=jnp.float32) * scaling
    later = lax.broadcasted_iota(jnp.int32, recent.shape, 1)
    second = lax.broadcasted_iota(jnp.int32, recent.shape, 0) >= recent.shape[0] // 2
    recent = jnp.where(later <= second.astype(jnp.int32), recent, -jnp.inf)
    highest = jnp.maximum(
        jnp.max(scores, axis=1, keepdims=True), jnp.max(recent, axis=1, keepdims=True)
    )
    far = jnp.exp(scores - highest)
    near = jnp.exp(recent - highest)
    inverse = 1.0 / (jnp.sum(far, axis=1, keepdims=True) + jnp.sum(near, axis=1, keepdims=True))
    combined = lax.dot_general(
        (far * inverse).astype(jnp.bfloat16),
        keys[:lat_width],
        flat,
        preferred_element_type=jnp.float32,
    ) + jnp.dot(
        (near * inverse).astype(jnp.bfloat16),
        own[:, :lat_width],
        preferred_element_type=jnp.float32,
    )
    out_ref[0] = combined.astype(out_ref.dtype)


def attend(cache, lo, hi, queries, own_keys, lat_width, width, scaling):
    number, steps, heads, wide = queries.shape
    shared = cache.shape[0] == 1
    own_keys = jnp.pad(own_keys, ((0, 0), (0, 16 - steps), (0, 0)))
    out = pl.pallas_call(
        lambda *refs: attend_kernel(width, scaling, *refs),
        grid_spec=pltpu.PrefetchScalarGridSpec(
            num_scalar_prefetch=2,
            grid=(number,),
            in_specs=[
                pl.BlockSpec((1, steps * heads, wide), lambda r, lo, hi: (r, 0, 0)),
                pl.BlockSpec((1, 16, wide), lambda r, lo, hi: (r, 0, 0)),
                pl.BlockSpec(
                    (1,) + cache.shape[1:], lambda r, lo, hi: (0 if shared else r, 0, 0)
                ),
            ],
            out_specs=pl.BlockSpec((1, steps * heads, lat_width), lambda r, lo, hi: (r, 0, 0)),
        ),
        out_shape=jax.ShapeDtypeStruct((number, steps * heads, lat_width), jnp.bfloat16),
        compiler_params=pltpu.CompilerParams(vmem_limit_bytes=24 * 2**20),
        cost_estimate=pl.CostEstimate(
            flops=4 * number * steps * heads * wide * width,
            bytes_accessed=2 * (cache.size + 2 * queries.size),
            transcendentals=number * steps * heads * width,
        ),
    )(lo, hi, queries.reshape(number, steps * heads, wide), own_keys, cache)
    return out.reshape(number, steps, heads, lat_width)


WIDE = 2


def flip(index, bits):
    for bit in (1, 2, 4):
        if bits & bit:
            index = index + bit - 2 * bit * lax.rem(lax.div(index, bit), 2)
    return index


def exchange_old(rows):
    everyone = range(lax.axis_size("pool"))
    swap = lambda block, n: lax.ppermute(block, "pool", [(i, i ^ n) for i in everyone])
    across = {0: rows}
    for n in (2, 4, 6):
        across[n] = swap(rows, n)
    for n in (0, 2, 4, 6):
        across[n + 1] = swap(across[n], 1)
    return [across[n] for n in everyone]


def gather_out_kernel(
    high,
    h_ref,
    old_hbm,
    w_hbm,
    fresh_ref,
    old_ref,
    blocks,
    old_rows,
    weight,
    total,
    land_fresh,
    land_old,
    recv_sem,
    send_sem,
    local_sem,
    pair_send,
    pair_recv,
):
    me = lax.axis_index("pool")
    core = lax.axis_index("tp")
    row = lax.div(me, WIDE)
    col = lax.rem(me, WIDE)
    side = row * WIDE + (1 - col)
    up, down = me + WIDE, me - WIDE
    has_up, has_down = row < high - 1, row > 0
    w_copy = pltpu.make_async_copy(w_hbm, weight, local_sem.at[0])
    w_copy.start()
    own_copy = pltpu.make_async_copy(h_ref, blocks.at[me], local_sem.at[1])
    old_copies = []
    for n, ref in enumerate(old_hbm):
        owner = flip(me, n)
        old_copies.append(pltpu.make_async_copy(ref, old_rows.at[owner], local_sem.at[2 + n]))
        old_copies[-1].start()

    barrier = pltpu.get_barrier_semaphore()

    def greet(target):
        pl.semaphore_signal(
            barrier, inc=1, device_id=target, device_id_type=pl.DeviceIdType.MESH
        )

    greet({"pool": side})
    greet({"tp": 1 - core})
    pl.when(has_up)(lambda: greet({"pool": up}))
    pl.when(has_down)(lambda: greet({"pool": down}))
    pl.semaphore_wait(barrier, 2 + has_up.astype(jnp.int32) + has_down.astype(jnp.int32))

    def copy(slot, way, own=False):
        return pltpu.make_async_remote_copy(
            src_ref=h_ref if own else blocks.at[slot],
            dst_ref=blocks.at[slot],
            send_sem=send_sem.at[slot, way],
            recv_sem=recv_sem.at[slot],
            device_id={"pool": (side, up, down)[way]},
            device_id_type=pl.DeviceIdType.MESH,
        )

    def pair_copy(n, src, dst):
        return pltpu.make_async_remote_copy(
            src_ref=src,
            dst_ref=dst,
            send_sem=pair_send.at[n],
            recv_sem=pair_recv.at[n],
            device_id={"tp": 1 - core},
            device_id_type=pl.DeviceIdType.MESH,
        )

    pl.when(has_up)(lambda: copy(me, 1, True).start())
    pl.when(has_down)(lambda: copy(me, 2, True).start())
    copy(me, 0, True).start()
    own_copy.start()
    total[...] = jnp.zeros_like(total)
    slots, rows, depth = blocks.shape
    part = depth // 8
    half_rows, half_slots = rows // 2, slots // 2
    w_copy.wait()
    for one in old_copies:
        one.wait()

    def multiply(piece, source, first, last):
        @pl.loop(first, last)
        def _(k):
            cut = pl.ds(pl.multiple_of(k * part, part), part)
            left = source[:, :, cut].reshape(slots * rows, part)
            total[piece] += jnp.dot(
                left, weight[cut, :], preferred_element_type=jnp.float32
            ).reshape(total.shape[1:])

    bounds = [8 * n // high for n in range(high + 1)]
    for step in range(1, high):
        multiply(1, old_rows, bounds[step - 1], bounds[step])

        @pl.when(row >= step)
        def _():
            slot = me - step * WIDE
            copy(slot, 0).wait_recv()
            pl.when(has_up)(lambda: copy(slot, 1).start())
            copy(slot, 0).start()

        @pl.when(row + step < high)
        def _():
            slot = me + step * WIDE
            copy(slot, 0).wait_recv()
            pl.when(has_down)(lambda: copy(slot, 2).start())
            copy(slot, 0).start()

    multiply(1, old_rows, bounds[high - 1], 8)
    old_pair = pair_copy(1, total.at[1, pl.ds((1 - core) * half_slots, half_slots)], land_old)
    old_pair.start()
    own_copy.wait()
    for at in range(high):
        copy(at * WIDE + 1 - col, 0).wait_recv()
    multiply(0, blocks, 0, 8)
    their_rows = pl.ds(pl.multiple_of((1 - core) * half_rows, half_rows), half_rows)
    my_rows = pl.ds(pl.multiple_of(core * half_rows, half_rows), half_rows)
    fresh_pair = pair_copy(0, total.at[0, :, their_rows, :], land_fresh)
    fresh_pair.start()
    old_pair.wait()
    old_ref[...] = (total[1, pl.ds(core * half_slots, half_slots)] + land_old[...]).astype(
        old_ref.dtype
    )
    fresh_pair.wait()
    fresh_ref[...] = (total[0, :, my_rows, :] + land_fresh[...]).astype(fresh_ref.dtype)

    copy(me, 0, True).wait_send()
    pl.when(has_up)(lambda: copy(me, 1, True).wait_send())
    pl.when(has_down)(lambda: copy(me, 2, True).wait_send())
    for step in range(1, high):

        @pl.when(row >= step)
        def _():
            slot = me - step * WIDE
            pl.when(has_up)(lambda: copy(slot, 1).wait_send())
            copy(slot, 0).wait_send()

        @pl.when(row + step < high)
        def _():
            slot = me + step * WIDE
            pl.when(has_down)(lambda: copy(slot, 2).wait_send())
            copy(slot, 0).wait_send()


def gather_out(fresh_rows, old_rows, n_old, out_weight):
    pool = lax.axis_size("pool")
    rows = 2 * pool
    depth, cols = out_weight.shape
    fresh, old = pl.pallas_call(
        lambda h, *refs: gather_out_kernel(
            pool // WIDE, h, refs[:pool], refs[pool], *refs[pool + 1 :]
        ),
        out_shape=(
            jax.ShapeDtypeStruct((pool, rows // 2, cols), jnp.float32),
            jax.ShapeDtypeStruct((pool // 2, rows, cols), jnp.float32),
        ),
        in_specs=[
            pl.BlockSpec(memory_space=pltpu.VMEM),
            *[pl.BlockSpec(memory_space=pl.ANY)] * (pool + 1),
        ],
        out_specs=[pl.BlockSpec(memory_space=pltpu.VMEM)] * 2,
        scratch_shapes=[
            pltpu.VMEM((pool, rows, depth), jnp.bfloat16),
            pltpu.VMEM((pool, rows, depth), jnp.bfloat16),
            pltpu.VMEM((depth, cols), jnp.bfloat16),
            pltpu.VMEM((2, pool, rows, cols), jnp.float32),
            pltpu.VMEM((pool, rows // 2, cols), jnp.float32),
            pltpu.VMEM((pool // 2, rows, cols), jnp.float32),
            pltpu.SemaphoreType.DMA((pool,)),
            pltpu.SemaphoreType.DMA((pool, 3)),
            pltpu.SemaphoreType.DMA((2 + pool,)),
            pltpu.SemaphoreType.DMA((2,)),
            pltpu.SemaphoreType.DMA((2,)),
        ],
        compiler_params=pltpu.CompilerParams(
            collective_id=0, has_side_effects=True, vmem_limit_bytes=40 * 2**20
        ),
    )(fresh_rows, *old_rows, out_weight)
    fresh = fresh.reshape(pool, pool // 2, 2, cols).transpose(1, 0, 2, 3)
    old = old[:, :n_old].reshape(pool // 2, n_old // 2, 2, cols)
    return jnp.concatenate([fresh, old], axis=1).reshape(-1, cols).astype(jnp.bfloat16)


def body(
    x_pre,
    x_dec,
    q_dec,
    kv_weight,
    kv_gain,
    up_key,
    up_value,
    out_weight,
    old_cache,
    old_lens,
    prompt_lens,
    owners,
):
    pool_size = lax.axis_size("pool")
    own_pool = lax.axis_index("pool")
    requests = x_dec.shape[0]
    model_part = x_pre.shape[1]
    heads_here = up_key.shape[0]
    lat_width = kv_gain.shape[0]
    scaling = 1.0 / math.sqrt(NOPE + ROPE)

    query_cols = q_dec.shape[-1]
    sent = jnp.concatenate([q_dec[:pool_size], x_dec[:pool_size]], axis=-1)
    arrived = lax.all_to_all(sent, "pool", split_axis=0, concat_axis=0, tiled=True)
    fresh_q, fresh_x = arrived[..., :query_cols], arrived[..., query_cols:]

    x_rows = jnp.concatenate([fresh_x, x_dec[pool_size:]], axis=0).reshape(-1, model_part)
    dec_raw = tp_sum(jnp.dot(x_rows, kv_weight, preferred_element_type=jnp.float32))
    dec_keys = normalize(dec_raw, kv_gain).reshape(requests, 2, -1)
    q_rows = jnp.concatenate([fresh_q, q_dec[pool_size:]], axis=0).reshape(
        requests, 2, heads_here, NOPE + ROPE
    )
    absorbed = jnp.einsum(
        "rihn,hnc->rihc", q_rows[..., :NOPE], up_key, preferred_element_type=jnp.float32
    )
    full_query = jnp.concatenate([absorbed.astype(jnp.bfloat16), q_rows[..., NOPE:]], axis=-1)

    def lift(combined):
        return (
            jnp.einsum("rihc,hcv->rihv", combined, up_value, preferred_element_type=jnp.float32)
            .astype(jnp.bfloat16)
            .reshape(combined.shape[0] * 2, -1)
        )

    old_rows = lift(
        attend(
            old_cache.transpose(0, 2, 1),
            jnp.zeros_like(old_lens),
            old_lens,
            full_query[pool_size:],
            dec_keys[pool_size:],
            lat_width,
            old_cache.shape[1],
            scaling,
        )
    )
    n_old = old_rows.shape[0]
    old_rows = jnp.pad(old_rows, ((0, 2 * pool_size - n_old), (0, 0)))
    small = lax.axis_size("tp") == 2 and pool_size == 8
    if small:
        all_old = exchange_old(old_rows)
    else:
        all_old = lax.all_gather(old_rows, "pool", axis=0, tiled=False)

    chunks = 4
    rows = x_pre.shape[0] // chunks
    late_weight, _ = lax.optimization_barrier((kv_weight, old_rows))
    pre_rows = jnp.concatenate(
        [
            normalize(
                tp_sum(
                    jnp.dot(
                        x_pre[c * rows : (c + 1) * rows],
                        late_weight if c else kv_weight,
                        preferred_element_type=jnp.float32,
                    )
                ),
                kv_gain,
            )
            for c in range(chunks)
        ],
        axis=0,
    )

    my_lengths = lax.dynamic_index_in_dim(prompt_lens, own_pool, 0, keepdims=False)
    my_owners = lax.dynamic_index_in_dim(owners, own_pool, 0, keepdims=False)
    targets = jnp.arange(pool_size, dtype=jnp.int32)
    chosen = my_owners[:, None] == targets[None, :]
    begins = jnp.cumsum(my_lengths) - my_lengths
    start = jnp.sum(jnp.where(chosen, begins[:, None], 0), axis=0)
    count = jnp.sum(jnp.where(chosen, my_lengths[:, None], 0), axis=0)
    longest = 2 * x_pre.shape[0] // pool_size
    window = min(-(-longest // 128) * 128 + 128, x_pre.shape[0])
    fresh_rows = lift(
        attend(
            pre_rows.T[None],
            start,
            start + count,
            full_query[:pool_size],
            dec_keys[:pool_size],
            lat_width,
            window,
            scaling,
        )
    )
    if small:
        return gather_out(fresh_rows, all_old, n_old, out_weight)
    all_fresh = lax.all_gather(fresh_rows, "pool", axis=0, tiled=False)
    partial_out = jnp.dot(
        jnp.concatenate([all_fresh, all_old], axis=1), out_weight, preferred_element_type=jnp.float32
    )
    cols = partial_out.shape[-1]
    partial_out = partial_out.reshape(pool_size, 2 * pool_size, 2, cols)
    partial_out = jnp.concatenate(
        [
            partial_out[:, :pool_size].transpose(1, 0, 2, 3),
            partial_out[:, pool_size : pool_size + n_old // 2],
        ],
        axis=1,
    ).reshape(-1, cols)
    return tp_scatter(partial_out).astype(jnp.bfloat16)


def solution(mesh):
    placed = (
        P(("groups", "pool"), "tp"),
        P(("groups", "pool"), None, "tp"),
        P(("groups", "pool"), None, "tp"),
        P("tp", None),
        P(),
        P("tp", None, None),
        P("tp", None, None),
        P("tp", "pool"),
        P(("groups", "pool"), None, None),
        P(("groups", "pool")),
        P("groups", None),
        P("groups", None),
    )
    return jax.shard_map(
        body, mesh=mesh, in_specs=placed, out_specs=P(("groups", "tp"), "pool"), check_vma=False
    )
```

```python
import math

import jax
import jax.numpy as jnp
from jax import lax
from jax.experimental import pallas as pl
from jax.experimental.pallas import tpu as pltpu
from jax.sharding import PartitionSpec as P

ROPE = 64
NOPE = 128


def normalize(raw_rows, kv_gain):
    lat_width = kv_gain.shape[0]
    rest = raw_rows.shape[-1] - lat_width
    latent = raw_rows[..., :lat_width]
    factor = lax.rsqrt(jnp.mean(latent * latent, axis=-1, keepdims=True) + 1e-06)
    inside = jnp.arange(raw_rows.shape[-1]) < lat_width
    gain = jnp.concatenate([kv_gain, jnp.ones((rest,), kv_gain.dtype)])
    return (raw_rows * jnp.where(inside, factor, 1.0) * gain).astype(jnp.bfloat16)


def tp_sum(part):
    if lax.axis_size("tp") == 2:
        return part + lax.ppermute(part, "tp", [(0, 1), (1, 0)])
    return lax.psum(part, "tp")


def tp_scatter(part):
    if lax.axis_size("tp") == 2:
        half = part.shape[0] // 2
        me = lax.axis_index("tp")
        mine = lax.dynamic_slice_in_dim(part, me * half, half, 0)
        other = lax.dynamic_slice_in_dim(part, (1 - me) * half, half, 0)
        return mine + lax.ppermute(other, "tp", [(0, 1), (1, 0)])
    return lax.psum_scatter(part, "tp", scatter_dimension=0, tiled=True)


def attend_kernel(width, scaling, lo_ref, hi_ref, q_ref, own_ref, cache_ref, out_ref):
    at = pl.program_id(0)
    lo, hi = lo_ref[at], hi_ref[at]
    lat_width = out_ref.shape[-1]
    room = cache_ref.shape[-1] - width
    base = pl.multiple_of(jnp.minimum(lax.div(lo, 128) * 128, room), 128) if room else 0
    query = q_ref[0]
    own = own_ref[0]
    keys = cache_ref[0, :, pl.ds(base, width)]
    scores = jnp.dot(query, keys, preferred_element_type=jnp.float32) * scaling
    places = base + lax.broadcasted_iota(jnp.int32, scores.shape, 1)
    scores = jnp.where((places >= lo) & (places < hi), scores, -jnp.inf)
    flat = (((1,), (1,)), ((), ()))
    recent = lax.dot_general(query, own, flat, preferred_element_type=jnp.float32) * scaling
    later = lax.broadcasted_iota(jnp.int32, recent.shape, 1)
    second = lax.broadcasted_iota(jnp.int32, recent.shape, 0) >= recent.shape[0] // 2
    recent = jnp.where(later <= second.astype(jnp.int32), recent, -jnp.inf)
    highest = jnp.maximum(
        jnp.max(scores, axis=1, keepdims=True), jnp.max(recent, axis=1, keepdims=True)
    )
    far = jnp.exp(scores - highest)
    near = jnp.exp(recent - highest)
    inverse = 1.0 / (jnp.sum(far, axis=1, keepdims=True) + jnp.sum(near, axis=1, keepdims=True))
    combined = lax.dot_general(
        (far * inverse).astype(jnp.bfloat16),
        keys[:lat_width],
        flat,
        preferred_element_type=jnp.float32,
    ) + jnp.dot(
        (near * inverse).astype(jnp.bfloat16),
        own[:, :lat_width],
        preferred_element_type=jnp.float32,
    )
    out_ref[0] = combined.astype(out_ref.dtype)


def attend(cache, lo, hi, queries, own_keys, lat_width, width, scaling):
    number, steps, heads, wide = queries.shape
    shared = cache.shape[0] == 1
    own_keys = jnp.pad(own_keys, ((0, 0), (0, 16 - steps), (0, 0)))
    out = pl.pallas_call(
        lambda *refs: attend_kernel(width, scaling, *refs),
        grid_spec=pltpu.PrefetchScalarGridSpec(
            num_scalar_prefetch=2,
            grid=(number,),
            in_specs=[
                pl.BlockSpec((1, steps * heads, wide), lambda r, lo, hi: (r, 0, 0)),
                pl.BlockSpec((1, 16, wide), lambda r, lo, hi: (r, 0, 0)),
                pl.BlockSpec(
                    (1,) + cache.shape[1:], lambda r, lo, hi: (0 if shared else r, 0, 0)
                ),
            ],
            out_specs=pl.BlockSpec((1, steps * heads, lat_width), lambda r, lo, hi: (r, 0, 0)),
        ),
        out_shape=jax.ShapeDtypeStruct((number, steps * heads, lat_width), jnp.bfloat16),
        compiler_params=pltpu.CompilerParams(vmem_limit_bytes=24 * 2**20),
        cost_estimate=pl.CostEstimate(
            flops=4 * number * steps * heads * wide * width,
            bytes_accessed=2 * (cache.size + 2 * queries.size),
            transcendentals=number * steps * heads * width,
        ),
    )(lo, hi, queries.reshape(number, steps * heads, wide), own_keys, cache)
    return out.reshape(number, steps, heads, lat_width)


WIDE = 2


def flip(index, bits):
    for bit in (1, 2, 4):
        if bits & bit:
            index = index + bit - 2 * bit * lax.rem(lax.div(index, bit), 2)
    return index


def exchange_old(rows):
    everyone = range(lax.axis_size("pool"))
    swap = lambda block, n: lax.ppermute(block, "pool", [(i, i ^ n) for i in everyone])
    across = {0: rows}
    for n in (2, 4, 6):
        across[n] = swap(rows, n)
    for n in (0, 2, 4, 6):
        across[n + 1] = swap(across[n], 1)
    return [across[n] for n in everyone]


def gather_out_kernel(
    high,
    h_ref,
    old_hbm,
    w_hbm,
    fresh_ref,
    old_ref,
    blocks,
    old_rows,
    weight,
    total,
    land_fresh,
    land_old,
    recv_sem,
    send_sem,
    local_sem,
    pair_send,
    pair_recv,
):
    me = lax.axis_index("pool")
    core = lax.axis_index("tp")
    row = lax.div(me, WIDE)
    col = lax.rem(me, WIDE)
    side = row * WIDE + (1 - col)
    up, down = me + WIDE, me - WIDE
    has_up, has_down = row < high - 1, row > 0
    w_copy = pltpu.make_async_copy(w_hbm, weight, local_sem.at[0])
    w_copy.start()
    own_copy = pltpu.make_async_copy(h_ref, blocks.at[me], local_sem.at[1])
    old_copies = []
    for n, ref in enumerate(old_hbm):
        owner = flip(me, n)
        old_copies.append(pltpu.make_async_copy(ref, old_rows.at[owner], local_sem.at[2 + n]))
        old_copies[-1].start()

    barrier = pltpu.get_barrier_semaphore()

    def greet(target):
        pl.semaphore_signal(
            barrier, inc=1, device_id=target, device_id_type=pl.DeviceIdType.MESH
        )

    greet({"pool": side})
    greet({"tp": 1 - core})
    pl.when(has_up)(lambda: greet({"pool": up}))
    pl.when(has_down)(lambda: greet({"pool": down}))
    pl.semaphore_wait(barrier, 2 + has_up.astype(jnp.int32) + has_down.astype(jnp.int32))

    def copy(slot, way, own=False):
        return pltpu.make_async_remote_copy(
            src_ref=h_ref if own else blocks.at[slot],
            dst_ref=blocks.at[slot],
            send_sem=send_sem.at[slot, way],
            recv_sem=recv_sem.at[slot],
            device_id={"pool": (side, up, down)[way]},
            device_id_type=pl.DeviceIdType.MESH,
        )

    def pair_copy(n, src, dst):
        return pltpu.make_async_remote_copy(
            src_ref=src,
            dst_ref=dst,
            send_sem=pair_send.at[n],
            recv_sem=pair_recv.at[n],
            device_id={"tp": 1 - core},
            device_id_type=pl.DeviceIdType.MESH,
        )

    pl.when(has_up)(lambda: copy(me, 1, True).start())
    pl.when(has_down)(lambda: copy(me, 2, True).start())
    copy(me, 0, True).start()
    own_copy.start()
    total[...] = jnp.zeros_like(total)
    slots, rows, depth = blocks.shape
    part = depth // 8
    half_rows, half_slots = rows // 2, slots // 2
    w_copy.wait()
    for one in old_copies:
        one.wait()

    def multiply(piece, source, first, last):
        @pl.loop(first, last)
        def _(k):
            cut = pl.ds(pl.multiple_of(k * part, part), part)
            left = source[:, :, cut].reshape(slots * rows, part)
            total[piece] += jnp.dot(
                left, weight[cut, :], preferred_element_type=jnp.float32
            ).reshape(total.shape[1:])

    bounds = [8 * n // high for n in range(high + 1)]
    for step in range(1, high):
        multiply(1, old_rows, bounds[step - 1], bounds[step])

        @pl.when(row >= step)
        def _():
            slot = me - step * WIDE
            copy(slot, 0).wait_recv()
            pl.when(has_up)(lambda: copy(slot, 1).start())
            copy(slot, 0).start()

        @pl.when(row + step < high)
        def _():
            slot = me + step * WIDE
            copy(slot, 0).wait_recv()
            pl.when(has_down)(lambda: copy(slot, 2).start())
            copy(slot, 0).start()

    multiply(1, old_rows, bounds[high - 1], 8)
    old_pair = pair_copy(1, total.at[1, pl.ds((1 - core) * half_slots, half_slots)], land_old)
    old_pair.start()
    own_copy.wait()
    for at in range(high):
        copy(at * WIDE + 1 - col, 0).wait_recv()
    multiply(0, blocks, 0, 8)
    their_rows = pl.ds(pl.multiple_of((1 - core) * half_rows, half_rows), half_rows)
    my_rows = pl.ds(pl.multiple_of(core * half_rows, half_rows), half_rows)
    fresh_pair = pair_copy(0, total.at[0, :, their_rows, :], land_fresh)
    fresh_pair.start()
    old_pair.wait()
    old_ref[...] = (total[1, pl.ds(core * half_slots, half_slots)] + land_old[...]).astype(
        old_ref.dtype
    )
    fresh_pair.wait()
    fresh_ref[...] = (total[0, :, my_rows, :] + land_fresh[...]).astype(fresh_ref.dtype)

    copy(me, 0, True).wait_send()
    pl.when(has_up)(lambda: copy(me, 1, True).wait_send())
    pl.when(has_down)(lambda: copy(me, 2, True).wait_send())
    for step in range(1, high):

        @pl.when(row >= step)
        def _():
            slot = me - step * WIDE
            pl.when(has_up)(lambda: copy(slot, 1).wait_send())
            copy(slot, 0).wait_send()

        @pl.when(row + step < high)
        def _():
            slot = me + step * WIDE
            pl.when(has_down)(lambda: copy(slot, 2).wait_send())
            copy(slot, 0).wait_send()


def gather_out(fresh_rows, old_rows, n_old, out_weight):
    pool = lax.axis_size("pool")
    rows = 2 * pool
    depth, cols = out_weight.shape
    fresh, old = pl.pallas_call(
        lambda h, *refs: gather_out_kernel(
            pool // WIDE, h, refs[:pool], refs[pool], *refs[pool + 1 :]
        ),
        out_shape=(
            jax.ShapeDtypeStruct((pool, rows // 2, cols), jnp.float32),
            jax.ShapeDtypeStruct((pool // 2, rows, cols), jnp.float32),
        ),
        in_specs=[
            pl.BlockSpec(memory_space=pltpu.VMEM),
            *[pl.BlockSpec(memory_space=pl.ANY)] * (pool + 1),
        ],
        out_specs=[pl.BlockSpec(memory_space=pltpu.VMEM)] * 2,
        scratch_shapes=[
            pltpu.VMEM((pool, rows, depth), jnp.bfloat16),
            pltpu.VMEM((pool, rows, depth), jnp.bfloat16),
            pltpu.VMEM((depth, cols), jnp.bfloat16),
            pltpu.VMEM((2, pool, rows, cols), jnp.float32),
            pltpu.VMEM((pool, rows // 2, cols), jnp.float32),
            pltpu.VMEM((pool // 2, rows, cols), jnp.float32),
            pltpu.SemaphoreType.DMA((pool,)),
            pltpu.SemaphoreType.DMA((pool, 3)),
            pltpu.SemaphoreType.DMA((2 + pool,)),
            pltpu.SemaphoreType.DMA((2,)),
            pltpu.SemaphoreType.DMA((2,)),
        ],
        compiler_params=pltpu.CompilerParams(
            collective_id=0, has_side_effects=True, vmem_limit_bytes=40 * 2**20
        ),
    )(fresh_rows, *old_rows, out_weight)
    fresh = fresh.reshape(pool, pool // 2, 2, cols).transpose(1, 0, 2, 3)
    old = old[:, :n_old].reshape(pool // 2, n_old // 2, 2, cols)
    return jnp.concatenate([fresh, old], axis=1).reshape(-1, cols).astype(jnp.bfloat16)


def body(
    x_pre,
    x_dec,
    q_dec,
    kv_weight,
    kv_gain,
    up_key,
    up_value,
    out_weight,
    old_cache,
    old_lens,
    prompt_lens,
    owners,
):
    pool_size = lax.axis_size("pool")
    own_pool = lax.axis_index("pool")
    requests = x_dec.shape[0]
    model_part = x_pre.shape[1]
    heads_here = up_key.shape[0]
    lat_width = kv_gain.shape[0]
    scaling = 1.0 / math.sqrt(NOPE + ROPE)

    query_cols = q_dec.shape[-1]
    sent = jnp.concatenate([q_dec[:pool_size], x_dec[:pool_size]], axis=-1)
    arrived = lax.all_to_all(sent, "pool", split_axis=0, concat_axis=0, tiled=True)
    early_weight, _ = lax.optimization_barrier((kv_weight, sent))
    chunks = 4
    rows = x_pre.shape[0] // chunks

    def prefill(c, weight):
        return jnp.dot(
            x_pre[c * rows : (c + 1) * rows], weight, preferred_element_type=jnp.float32
        )

    parts = [prefill(c, early_weight) for c in range(2)]
    arrived, *parts = lax.optimization_barrier((arrived, *parts))
    fresh_q, fresh_x = arrived[..., :query_cols], arrived[..., query_cols:]

    x_rows = jnp.concatenate([fresh_x, x_dec[pool_size:]], axis=0).reshape(-1, model_part)
    dec_raw = tp_sum(jnp.dot(x_rows, kv_weight, preferred_element_type=jnp.float32))
    dec_keys = normalize(dec_raw, kv_gain).reshape(requests, 2, -1)
    q_rows = jnp.concatenate([fresh_q, q_dec[pool_size:]], axis=0).reshape(
        requests, 2, heads_here, NOPE + ROPE
    )
    absorbed = jnp.einsum(
        "rihn,hnc->rihc", q_rows[..., :NOPE], up_key, preferred_element_type=jnp.float32
    )
    full_query = jnp.concatenate([absorbed.astype(jnp.bfloat16), q_rows[..., NOPE:]], axis=-1)

    def lift(combined):
        return (
            jnp.einsum("rihc,hcv->rihv", combined, up_value, preferred_element_type=jnp.float32)
            .astype(jnp.bfloat16)
            .reshape(combined.shape[0] * 2, -1)
        )

    old_rows = lift(
        attend(
            old_cache.transpose(0, 2, 1),
            jnp.zeros_like(old_lens),
            old_lens,
            full_query[pool_size:],
            dec_keys[pool_size:],
            lat_width,
            old_cache.shape[1],
            scaling,
        )
    )
    n_old = old_rows.shape[0]
    old_rows = jnp.pad(old_rows, ((0, 2 * pool_size - n_old), (0, 0)))
    small = lax.axis_size("tp") == 2 and pool_size == 8
    if small:
        all_old = exchange_old(old_rows)
    else:
        all_old = lax.all_gather(old_rows, "pool", axis=0, tiled=False)

    late_weight, _ = lax.optimization_barrier((kv_weight, old_rows))
    parts += [prefill(c, late_weight) for c in range(2, chunks)]
    pre_rows = jnp.concatenate([normalize(tp_sum(part), kv_gain) for part in parts], axis=0)

    my_lengths = lax.dynamic_index_in_dim(prompt_lens, own_pool, 0, keepdims=False)
    my_owners = lax.dynamic_index_in_dim(owners, own_pool, 0, keepdims=False)
    targets = jnp.arange(pool_size, dtype=jnp.int32)
    chosen = my_owners[:, None] == targets[None, :]
    begins = jnp.cumsum(my_lengths) - my_lengths
    start = jnp.sum(jnp.where(chosen, begins[:, None], 0), axis=0)
    count = jnp.sum(jnp.where(chosen, my_lengths[:, None], 0), axis=0)
    longest = 2 * x_pre.shape[0] // pool_size
    window = min(-(-longest // 128) * 128 + 128, x_pre.shape[0])
    fresh_rows = lift(
        attend(
            pre_rows.T[None],
            start,
            start + count,
            full_query[:pool_size],
            dec_keys[:pool_size],
            lat_width,
            window,
            scaling,
        )
    )
    if small:
        return gather_out(fresh_rows, all_old, n_old, out_weight)
    all_fresh = lax.all_gather(fresh_rows, "pool", axis=0, tiled=False)
    partial_out = jnp.dot(
        jnp.concatenate([all_fresh, all_old], axis=1), out_weight, preferred_element_type=jnp.float32
    )
    cols = partial_out.shape[-1]
    partial_out = partial_out.reshape(pool_size, 2 * pool_size, 2, cols)
    partial_out = jnp.concatenate(
        [
            partial_out[:, :pool_size].transpose(1, 0, 2, 3),
            partial_out[:, pool_size : pool_size + n_old // 2],
        ],
        axis=1,
    ).reshape(-1, cols)
    return tp_scatter(partial_out).astype(jnp.bfloat16)


def solution(mesh):
    placed = (
        P(("groups", "pool"), "tp"),
        P(("groups", "pool"), None, "tp"),
        P(("groups", "pool"), None, "tp"),
        P("tp", None),
        P(),
        P("tp", None, None),
        P("tp", None, None),
        P("tp", "pool"),
        P(("groups", "pool"), None, None),
        P(("groups", "pool")),
        P("groups", None),
        P("groups", None),
    )
    return jax.shard_map(
        body, mesh=mesh, in_specs=placed, out_specs=P(("groups", "tp"), "pool"), check_vma=False
    )
```
